32 devices in a mesh: row: 4 (over x, core), col: 8 (over z, y).
Axes of the slice: x: 2, y: 2, z: 4, core: 2. Of those that a mesh axis runs over, the one named last changes fastest.
Arguments:
- right_sides: bfloat16 [16384, 6144], P('row', 'col'), may hold values from -6 to 6
- factor_panels: bfloat16 [16384, 1024], P(('row', 'col')), may hold values from -0.1875 to 0.1875
- inverse_blocks: float32 [4, 256, 256], replicated, may hold values from -1 to 1, as said below
Outputs:
- solved_sides: float32 [16384, 6144], P('row', 'col')
The draws below stay inside these ranges and needn't reach their ends.
Inputs may be any that keep to these rules, and one draw needn't show every extreme that they name: `inverse_blocks`: each block is unit lower triangular.
All inputs are finite; a program needn't handle non-finite values.
Results may differ from the reference program's by a relative error of at most 0.003.
Values may be sent and summed in bfloat16 or wider, within the bound.
A program may use at most 192 MiB of HBM per device.

```python
import jax
import jax.numpy as jnp
from jax import lax

BS = 256
PANELS = 4
MB_DEV = 16
NRHS_DEV = 768
NR = 16384
NRHS = 6144
N_COL = 8


def draw_inverse_blocks(key, part):
    strict_part = jnp.clip(jax.random.normal(key, (PANELS, BS, BS), jnp.float32), -4.0, 4.0)
    strict_part = strict_part / jnp.sqrt(jnp.float32(BS))
    below_mask = jnp.tril(jnp.ones((BS, BS), jnp.float32), -1)
    return strict_part * below_mask + jnp.eye(BS, dtype=jnp.float32)


def shard_levels(stream_key, dims, split, least, high):
    level, own = 1.0, jax.random.fold_in(stream_key, 6)
    for dim, parts in split:
        steps = jnp.exp(jax.random.uniform(jax.random.fold_in(own, dim), (parts,), jnp.float32, least / len(split), high / len(split)))
        level = level * jnp.repeat(steps, dims[dim] // parts).reshape([-1 if axis == dim else 1 for axis in range(len(dims))])
    return level


def scatter_about(own_key, extent, scale, most, shards=(), kind=jnp.bfloat16):
    gain = shard_levels(own_key, extent, shards, -0.22, 0.18) if shards else 1.0
    entries = jax.random.normal(own_key, extent, jnp.float32) * scale * gain
    return jnp.minimum(jnp.maximum(entries, -most), most).astype(kind)


def setup_inputs(seed: int = 0) -> dict:
    key_of = jax.random.split(jax.random.key(seed), 4)
    right_sides = scatter_about(key_of[0], (NR, NRHS), 1.0, 6.0, ((0, 4), (1, 8)))
    factor_panels = scatter_about(key_of[1], (NR, PANELS * BS), (PANELS * BS) ** -0.5, 0.1875, ((0, 32),))
    inverse_blocks = draw_inverse_blocks(jax.random.fold_in(key_of[3], 71), 0)
    return dict(right_sides=right_sides, factor_panels=factor_panels, inverse_blocks=inverse_blocks)


def solve_columns(column_group, factor_panels, inverse_blocks):
    current = column_group.astype(jnp.float32)
    factor = factor_panels.astype(jnp.float32)
    row_blocks = jnp.arange(NR, dtype=jnp.int32) // BS
    for panel_num in range(PANELS):
        offset = panel_num * MB_DEV * BS
        leading = lax.dynamic_slice_in_dim(current, offset, BS, 0)
        solved = jnp.dot(inverse_blocks[panel_num], leading, precision=lax.Precision.HIGHEST)
        rounded = lax.optimization_barrier(solved.astype(jnp.bfloat16))
        shared = rounded.astype(jnp.float32)
        update = jnp.dot(factor[:, panel_num * BS:(panel_num + 1) * BS], shared, precision=lax.Precision.HIGHEST)
        is_panel = (row_blocks % MB_DEV == 0) & (row_blocks // MB_DEV <= panel_num)
        current = current - jnp.where(is_panel[:, None], jnp.zeros_like(update), update)
        current = lax.dynamic_update_slice_in_dim(current, solved, offset, 0)
    return current


def reference(right_sides, factor_panels, inverse_blocks):
    groups = right_sides.reshape(NR, N_COL, NRHS_DEV).transpose(1, 0, 2)
    solved_groups = lax.map(lambda group_cols: solve_columns(group_cols, factor_panels, inverse_blocks), groups)
    return solved_groups.transpose(1, 0, 2).reshape(NR, NRHS)
```

```python
import functools

import jax
import jax.numpy as jnp
from jax import lax
from jax.experimental import pallas as pl
from jax.experimental.pallas import tpu as pltpu
from jax.sharding import PartitionSpec as P

MESH = pl.DeviceIdType.MESH
UP, DOWN, RIGHT, LEFT = range(4)


def every(*conditions):
    kept = [c for c in conditions if c is not True]
    if not kept:
        return True
    return functools.reduce(jnp.logical_and, kept)


def run_if(condition, action):
    if condition is True:
        action()
    else:
        pl.when(condition)(action)


def gather_and_solve(
    rows, layers, lanes, parts,
    rhs_ref, factor_ref, inverse_ref,
    gathered, shared, own_solved,
    lead, panel_rows,
    send_sem, recv_sem, lead_send, lead_recv, panel_send, panel_recv, local_sem,
):
    panels, width, _ = inverse_ref.shape
    depth = factor_ref.shape[0]
    piece = depth // parts
    row = lax.axis_index("row")
    col = lax.axis_index("col")
    z, y = col // lanes, col % lanes
    balanced = lanes == 2 and layers % 2 == 0 and parts % 2 == 0 and width * 2 <= depth
    half = parts // 2
    panel_parts = width // piece

    barrier = pltpu.get_barrier_semaphore()
    can = {UP: z + 1 < layers, DOWN: z >= 1, RIGHT: y + 1 < lanes, LEFT: y >= 1}
    shift = {UP: lanes, DOWN: -lanes, RIGHT: 1, LEFT: -1}
    for way in (UP, DOWN, RIGHT, LEFT):
        def greet(way=way):
            pl.semaphore_signal(barrier, inc=1, device_id=(row, col + shift[way]), device_id_type=MESH)
        run_if(can[way], greet)
    for off in range(1, rows):
        pl.semaphore_signal(barrier, inc=1, device_id=(lax.rem(row + off, rows), col), device_id_type=MESH)
    neighbours = sum(jnp.where(can[way], 1, 0) for way in (UP, DOWN, RIGHT, LEFT))
    pl.semaphore_wait(barrier, rows - 1 + neighbours)

    pending = []

    def place(source, q):
        return gathered.at[pl.ds(pl.multiple_of(source * depth + q * piece, piece), piece)]

    def copy_of(way, target, source, q, own):
        src = factor_ref.at[pl.ds(q * piece, piece)] if own else place(source, q)
        return pltpu.make_async_remote_copy(
            src_ref=src, dst_ref=place(source, q),
            send_sem=send_sem.at[way, source, q], recv_sem=recv_sem.at[source, q],
            device_id=(row, target), device_id_type=MESH,
        )

    def send(condition, way, target, source, q, own=False):
        run_if(condition, lambda: copy_of(way, target, source, q, own).start())
        pending.append((condition, lambda: copy_of(way, target, source, q, own).wait_send()))

    def arrive(condition, source, q):
        run_if(condition, lambda: copy_of(UP, col, source, q, False).wait_recv())

    def send_own(q):
        for way in (UP, DOWN, RIGHT, LEFT):
            send(can[way], way, col + shift[way], col, q, own=True)

    def send_lead(off):
        target = lax.rem(row + off, rows)
        return pltpu.make_async_remote_copy(
            src_ref=rhs_ref.at[pl.ds(0, width)], dst_ref=lead.at[row],
            send_sem=lead_send.at[off], recv_sem=lead_recv.at[row],
            device_id=(target, col), device_id_type=MESH,
        )

    def send_panel(k, off, q):
        target = lax.rem(row + off, rows)
        span = (pl.ds(q * piece, piece), pl.ds(0, k * width))
        return pltpu.make_async_remote_copy(
            src_ref=gathered.at[span], dst_ref=panel_rows.at[(k - 1,) + span],
            send_sem=panel_send.at[off, q], recv_sem=panel_recv.at[k - 1, q],
            device_id=(target, col), device_id_type=MESH,
        )

    send_own(0)
    send_own(1)
    owner = row < panels
    own_block = pltpu.make_async_copy(factor_ref, gathered.at[pl.ds(pl.multiple_of(col * depth, depth), depth)], local_sem.at[0])
    own_block.start()
    for off in range(1, rows):
        run_if(owner, lambda off=off: send_lead(off).start())
        pending.append((owner, lambda off=off: send_lead(off).wait_send()))
    own_lead = pltpu.make_async_copy(rhs_ref.at[pl.ds(0, width)], lead.at[lax.rem(row, panels)], local_sem.at[1])
    run_if(owner, own_lead.start)
    run_if(owner, own_lead.wait)
    own_block.wait()

    def exchange_panel(q):
        for k in range(1, panels):
            for off in range(1, rows):
                run_if(row == k, lambda k=k, off=off: send_panel(k, off, q).start())
                pending.append((row == k, lambda k=k, off=off: send_panel(k, off, q).wait_send()))

    def pass_on(q):
        for d in range(1, layers):
            below, above = z >= d, z + d < layers
            source = col - d * lanes
            arrive(below, source, q)
            send(every(below, can[UP]), UP, col + lanes, source, q)
            kept = z % 2 == 0 if balanced and d == 1 and q >= half else True
            for way in (RIGHT, LEFT):
                send(every(below, can[way], kept), way, col + shift[way], source, q)
            source_above = col + d * lanes
            arrive(above, source_above, q)
            send(every(above, can[DOWN]), DOWN, col - lanes, source_above, q)
            kept = z % 2 == 1 if balanced and d == 1 and q >= half else True
            for way in (RIGHT, LEFT):
                send(every(above, can[way], kept), way, col + shift[way], source_above, q)

    other = z * lanes + (lanes - 1 - y)
    for q in range(parts):
        if q + 2 < parts:
            send_own(q + 2)
        pass_on(q)
        if balanced:
            if 1 <= q <= panel_parts:
                arrive(y == 1, 0, q - 1)
                exchange_panel(q - 1)
            if q >= half:
                arrive(True, other, q)
                send(True, z % 2, col + lanes * (1 - 2 * (z % 2)), other, q)
    if not balanced:
        for q in range(parts):
            for s in range(1, lanes):
                for layer in range(layers):
                    from_left, from_right = y >= s, y + s < lanes
                    arrive(from_left, layer * lanes + y - s, q)
                    send(every(from_left, can[RIGHT]), RIGHT, col + 1, layer * lanes + y - s, q)
                    arrive(from_right, layer * lanes + y + s, q)
                    send(every(from_right, can[LEFT]), LEFT, col - 1, layer * lanes + y + s, q)
        for q in range(panel_parts):
            exchange_panel(q)

    for k in range(1, panels):
        def own_rows(k=k):
            span = (pl.ds(0, width), pl.ds(0, k * width))
            move = pltpu.make_async_copy(gathered.at[span], panel_rows.at[(k - 1,) + span], local_sem.at[2])
            move.start()
            move.wait()
        def other_rows(k=k):
            for q in range(panel_parts):
                send_panel(k, 1, q).wait_recv()
        run_if(row == k, own_rows)
        run_if(row != k, other_rows)
    for k in range(panels):
        def other_lead(k=k):
            pltpu.make_async_remote_copy(
                src_ref=lead.at[k], dst_ref=lead.at[k], send_sem=lead_send.at[0], recv_sem=lead_recv.at[k],
                device_id=(row, col), device_id_type=MESH,
            ).wait_recv()
        run_if(row != k, other_lead)

    tile = min(256, shared.shape[1])

    @pl.loop(0, shared.shape[1] // tile)
    def _(step):
        at = pl.ds(pl.multiple_of(step * tile, tile), tile)
        for k in range(panels):
            current = lead[k, :, at].astype(jnp.float32)
            if k:
                current = current - jnp.dot(
                    panel_rows[k - 1, :, : k * width], shared[: k * width, at], preferred_element_type=jnp.float32
                )
            solved = jnp.dot(
                inverse_ref[k], current, precision=lax.Precision.HIGHEST, preferred_element_type=jnp.float32
            )
            shared[k * width : (k + 1) * width, at] = solved.astype(jnp.bfloat16)

            def keep(solved=solved):
                own_solved[:, at] = solved
            run_if(row == k, keep)

    if balanced:
        for layer in range(layers):
            for q in range(parts):
                source = layer * lanes + (lanes - 1 - y)
                if layer == 0 and q < panel_parts:
                    arrive(y == 0, source, q)
                elif q >= half:
                    arrive(z != layer, source, q)
                else:
                    arrive(True, source, q)
    for condition, finish in pending:
        run_if(condition, finish)


def multiply(row_ref, rhs_ref, gathered_ref, shared_ref, solved_ref, out_ref):
    step = pl.program_id(0)
    width = solved_ref.shape[0]
    update = jnp.dot(gathered_ref[...], shared_ref[...], preferred_element_type=jnp.float32)
    out_ref[...] = rhs_ref[...].astype(jnp.float32) - update

    @pl.when(jnp.logical_and(step == 0, row_ref[0] == 1))
    def _():
        out_ref[:width] = solved_ref[...]


def per_device(rows, layers, lanes, right_sides, factor_panels, inverse_blocks):
    height, count = right_sides.shape
    panels, width, _ = inverse_blocks.shape
    depth, across = factor_panels.shape
    cols = layers * lanes
    parts = 4
    dma = pltpu.SemaphoreType.DMA
    anywhere = pl.BlockSpec(memory_space=pl.ANY)
    in_vmem = pl.BlockSpec(memory_space=pltpu.VMEM)
    gathered, shared, own_solved = pl.pallas_call(
        functools.partial(gather_and_solve, rows, layers, lanes, parts),
        out_shape=(
            jax.ShapeDtypeStruct((cols * depth, across), factor_panels.dtype),
            jax.ShapeDtypeStruct((panels * width, count), jnp.bfloat16),
            jax.ShapeDtypeStruct((width, count), jnp.float32),
        ),
        in_specs=[anywhere, anywhere, in_vmem],
        out_specs=(anywhere, in_vmem, in_vmem),
        scratch_shapes=[
            pltpu.VMEM((panels, width, count), right_sides.dtype),
            pltpu.VMEM((panels - 1, width, (panels - 1) * width), factor_panels.dtype),
            dma((4, cols, parts)), dma((cols, parts)),
            dma((rows,)), dma((panels,)), dma((rows, parts)), dma((panels, parts)), dma((3,)),
        ],
        compiler_params=pltpu.CompilerParams(
            collective_id=0, has_side_effects=True, vmem_limit_bytes=24 << 20
        ),
    )(right_sides, factor_panels, inverse_blocks)

    tile = 512
    is_owner = (lax.axis_index("row") < panels).astype(jnp.int32).reshape(1)
    return pl.pallas_call(
        multiply,
        out_shape=jax.ShapeDtypeStruct((height, count), jnp.float32),
        grid_spec=pltpu.PrefetchScalarGridSpec(
            num_scalar_prefetch=1,
            grid=(height // tile,),
            in_specs=[
                pl.BlockSpec((tile, count), lambda i, s: (i, 0)),
                pl.BlockSpec((tile, across), lambda i, s: (i, 0)),
                pl.BlockSpec((across, count), lambda i, s: (0, 0)),
                pl.BlockSpec((width, count), lambda i, s: (0, 0)),
            ],
            out_specs=pl.BlockSpec((tile, count), lambda i, s: (i, 0)),
        ),
        compiler_params=pltpu.CompilerParams(vmem_limit_bytes=32 << 20),
    )(is_owner, right_sides, gathered, shared, own_solved)


def solution(mesh):
    rows, cols = mesh.shape["row"], mesh.shape["col"]
    lanes = max(1, rows // 2)
    placed = (P("row", "col"), P(("row", "col"), None), P())
    return jax.shard_map(
        functools.partial(per_device, rows, cols // lanes, lanes),
        mesh=mesh, in_specs=placed, out_specs=P("row", "col"), check_vma=False,
    )
```

```python
import functools

import jax
import jax.numpy as jnp
from jax import lax
from jax.experimental import pallas as pl
from jax.experimental.pallas import tpu as pltpu
from jax.sharding import PartitionSpec as P

MESH = pl.DeviceIdType.MESH
UP, DOWN, RIGHT, LEFT = 0, 1, 2, 3


def every(*conditions):
    kept = [c for c in conditions if c is not True]
    if not kept:
        return True
    return functools.reduce(jnp.logical_and, kept)


def run_if(condition, action):
    if condition is True:
        action()
    else:
        pl.when(condition)(action)


def gather_and_solve(
    rows, layers, lanes, parts,
    rhs_ref, factor_ref, inverse_hbm,
    gathered, shared, own_solved, partial,
    inverse_ref, lead, panel_rows, factor_held, rhs_held,
    send_sem, recv_sem, lead_send, lead_recv, panel_send, panel_recv, local_sem,
):
    panels, width, _ = inverse_ref.shape
    depth = factor_ref.shape[0]
    piece = depth // parts
    row = lax.axis_index("row")
    col = lax.axis_index("col")
    z, y = col // lanes, col % lanes
    balanced = lanes == 2 and layers % 2 == 0 and parts % 2 == 0 and width * 2 <= depth
    half = parts // 2
    panel_parts = width // piece

    barrier = pltpu.get_barrier_semaphore()
    can = {UP: z + 1 < layers, DOWN: z >= 1, RIGHT: y + 1 < lanes, LEFT: y >= 1}
    shift = {UP: lanes, DOWN: -lanes, RIGHT: 1, LEFT: -1}
    for way in (UP, DOWN, RIGHT, LEFT):
        def greet(way=way):
            pl.semaphore_signal(barrier, inc=1, device_id=(row, col + shift[way]), device_id_type=MESH)
        run_if(can[way], greet)
    for off in range(1, rows):
        pl.semaphore_signal(barrier, inc=1, device_id=(lax.rem(row + off, rows), col), device_id_type=MESH)
    neighbours = sum(jnp.where(can[way], 1, 0) for way in (UP, DOWN, RIGHT, LEFT))
    pl.semaphore_wait(barrier, rows - 1 + neighbours)

    pending = []

    def place(source, q):
        return gathered.at[pl.ds(pl.multiple_of(source * depth + q * piece, piece), piece)]

    def copy_of(way, target, source, q, own):
        src = factor_ref.at[pl.ds(q * piece, piece)] if own else place(source, q)
        return pltpu.make_async_remote_copy(
            src_ref=src, dst_ref=place(source, q),
            send_sem=send_sem.at[way, source, q], recv_sem=recv_sem.at[source, q],
            device_id=(row, target), device_id_type=MESH,
        )

    def send(condition, way, target, source, q, own=False):
        run_if(condition, lambda: copy_of(way, target, source, q, own).start())
        pending.append((condition, lambda: copy_of(way, target, source, q, own).wait_send()))

    def arrive(condition, source, q):
        run_if(condition, lambda: copy_of(UP, col, source, q, False).wait_recv())

    def send_own(q):
        for way in (UP, DOWN, RIGHT, LEFT):
            send(can[way], way, col + shift[way], col, q, own=True)

    def send_lead(off):
        target = lax.rem(row + off, rows)
        return pltpu.make_async_remote_copy(
            src_ref=rhs_ref.at[pl.ds(0, width)], dst_ref=lead.at[row],
            send_sem=lead_send.at[off], recv_sem=lead_recv.at[row],
            device_id=(target, col), device_id_type=MESH,
        )

    def send_panel(k, off, q):
        target = lax.rem(row + off, rows)
        span = (pl.ds(q * piece, piece), pl.ds(0, k * width))
        return pltpu.make_async_remote_copy(
            src_ref=gathered.at[span], dst_ref=panel_rows.at[(k - 1,) + span],
            send_sem=panel_send.at[off, q], recv_sem=panel_recv.at[k - 1, q],
            device_id=(target, col), device_id_type=MESH,
        )

    send_own(0)
    send_own(1)
    owner = row < panels
    own_block = pltpu.make_async_copy(factor_ref, gathered.at[pl.ds(pl.multiple_of(col * depth, depth), depth)], local_sem.at[0])
    own_block.start()
    for off in range(1, rows):
        run_if(owner, lambda off=off: send_lead(off).start())
        pending.append((owner, lambda off=off: send_lead(off).wait_send()))
    own_lead = pltpu.make_async_copy(rhs_ref.at[pl.ds(0, width)], lead.at[lax.rem(row, panels)], local_sem.at[1])
    run_if(owner, own_lead.start)
    run_if(owner, own_lead.wait)
    fetch_inverse = pltpu.make_async_copy(inverse_hbm, inverse_ref, local_sem.at[3])
    fetch_inverse.start()
    own_block.wait()

    def exchange_panel(q):
        for k in range(1, panels):
            for off in range(1, rows):
                run_if(row == k, lambda k=k, off=off: send_panel(k, off, q).start())
                pending.append((row == k, lambda k=k, off=off: send_panel(k, off, q).wait_send()))

    turn = 1 - 2 * (z // (layers // 2))

    def pass_on(q):
        for d in range(1, layers):
            for side in (turn, -turn):
                layer = z + side * d
                onward = z - side
                inside = jnp.logical_and(layer >= 0, layer < layers)
                source = layer * lanes + y
                arrive(inside, source, q)
                go_on = jnp.logical_and(onward >= 0, onward < layers)
                send(every(inside, go_on), (side + 1) // 2, onward * lanes + y, source, q)
                kept = layer != partner if balanced and d == 1 and q >= half else True
                for way in (RIGHT, LEFT):
                    send(every(inside, can[way], kept), way, col + shift[way], source, q)

    partner = z + 1 - 2 * (z % 2)
    other = z * lanes + (lanes - 1 - y)
    for q in range(parts):
        if q + 2 < parts:
            send_own(q + 2)
        pass_on(q)
        if balanced:
            if 1 <= q <= panel_parts:
                arrive(y == 1, 0, q - 1)
                exchange_panel(q - 1)
    if balanced:
        for q in range(half, parts):
            arrive(True, other, q)
            send(True, z % 2, col + lanes * (1 - 2 * (z % 2)), other, q)
    else:
        for q in range(parts):
            for s in range(1, lanes):
                for layer in range(layers):
                    from_left, from_right = y >= s, y + s < lanes
                    arrive(from_left, layer * lanes + y - s, q)
                    send(every(from_left, can[RIGHT]), RIGHT, col + 1, layer * lanes + y - s, q)
                    arrive(from_right, layer * lanes + y + s, q)
                    send(every(from_right, can[LEFT]), LEFT, col - 1, layer * lanes + y + s, q)
        for q in range(panel_parts):
            exchange_panel(q)

    for k in range(1, panels):
        def own_rows(k=k):
            span = (pl.ds(0, width), pl.ds(0, k * width))
            move = pltpu.make_async_copy(gathered.at[span], panel_rows.at[(k - 1,) + span], local_sem.at[2])
            move.start()
            move.wait()
        def other_rows(k=k):
            for q in range(panel_parts):
                send_panel(k, 1, q).wait_recv()
        run_if(row == k, own_rows)
        run_if(row != k, other_rows)
    for k in range(panels):
        def other_lead(k=k):
            pltpu.make_async_remote_copy(
                src_ref=lead.at[k], dst_ref=lead.at[k], send_sem=lead_send.at[0], recv_sem=lead_recv.at[k],
                device_id=(row, col), device_id_type=MESH,
            ).wait_recv()
        run_if(row != k, other_lead)

    fetch_inverse.wait()
    tile = min(256, shared.shape[1])

    @pl.loop(0, shared.shape[1] // tile)
    def _(step):
        at = pl.ds(pl.multiple_of(step * tile, tile), tile)
        for k in range(panels):
            current = lead[k, :, at].astype(jnp.float32)
            if k:
                current = current - jnp.dot(
                    panel_rows[k - 1, :, : k * width], shared[: k * width, at], preferred_element_type=jnp.float32
                )
            solved = jnp.dot(
                inverse_ref[k], current, precision=lax.Precision.HIGHEST, preferred_element_type=jnp.float32
            )
            shared[k * width : (k + 1) * width, at] = solved.astype(jnp.bfloat16)

            def keep(solved=solved):
                own_solved[:, at] = solved
            run_if(row == k, keep)

    def fetch(layer, slot):
        at = pl.ds(pl.multiple_of((layer * lanes + y) * depth, depth), depth)
        return (
            pltpu.make_async_copy(gathered.at[at], factor_held.at[slot], local_sem.at[4 + slot]),
            pltpu.make_async_copy(rhs_ref.at[at], rhs_held.at[slot], local_sem.at[6 + slot]),
        )

    for copy in fetch(0, 0):
        copy.start()

    @pl.loop(0, layers)
    def _(layer):
        slot = lax.rem(layer, 2)

        @pl.when(layer + 1 < layers)
        def _():
            for copy in fetch(layer + 1, 1 - slot):
                copy.start()

        for copy in fetch(layer, slot):
            copy.wait()
        update = jnp.dot(factor_held[slot], shared[...], preferred_element_type=jnp.float32)
        partial[pl.ds(pl.multiple_of(layer * depth, depth), depth), :] = rhs_held[slot].astype(jnp.float32) - update

    def keep_solved():
        partial[:width] = own_solved[...]
    run_if(jnp.logical_and(owner, y == 0), keep_solved)

    if balanced:
        for layer in range(layers):
            for q in range(parts):
                source = layer * lanes + (lanes - 1 - y)
                if layer == 0 and q < panel_parts:
                    arrive(y == 0, source, q)
                elif q >= half:
                    arrive(z != layer, source, q)
                else:
                    arrive(True, source, q)
    for condition, finish in pending:
        run_if(condition, finish)


def multiply(panels, layers, lanes, rhs_ref, gathered_ref, shared_ref, solved_ref, partial_ref, out_ref, held, sem, part_sem):
    width = solved_ref.shape[0]
    depth = held.shape[1]
    owner = lax.axis_index("row") < panels
    y = lax.axis_index("col") % lanes
    others = lanes - 1
    steps = layers * others

    def hand_on(layer):
        at = pl.ds(pl.multiple_of((layer * lanes + y) * depth, depth), depth)
        return pltpu.make_async_copy(partial_ref.at[pl.ds(layer * depth, depth)], out_ref.at[at], part_sem.at[layer])

    def source_of(step):
        return (step // others) * lanes + lax.rem(y + 1 + lax.rem(step, others), lanes)

    def write(step, slot):
        at = pl.ds(pl.multiple_of(source_of(step) * depth, depth), depth)
        return pltpu.make_async_copy(held.at[slot], out_ref.at[at], sem.at[slot])

    for layer in range(layers):
        hand_on(layer).start()

    @pl.loop(0, steps)
    def _(step):
        slot = lax.rem(step, 2)

        @pl.when(step >= 2)
        def _():
            write(step - 2, slot).wait()

        source = source_of(step)
        at = pl.ds(pl.multiple_of(source * depth, depth), depth)
        update = jnp.dot(gathered_ref[at, :], shared_ref[...], preferred_element_type=jnp.float32)
        held[slot] = rhs_ref[at, :].astype(jnp.float32) - update

        @pl.when(jnp.logical_and(source == 0, owner))
        def _():
            held[slot, :width] = solved_ref[...]

        write(step, slot).start()

    for step in range(max(steps - 2, 0), steps):
        write(step, step % 2).wait()
    for layer in range(layers):
        hand_on(layer).wait()


def per_device(rows, layers, lanes, right_sides, factor_panels, inverse_blocks):
    height, count = right_sides.shape
    panels, width, _ = inverse_blocks.shape
    depth, across = factor_panels.shape
    cols = layers * lanes
    parts = 4
    dma = pltpu.SemaphoreType.DMA
    anywhere = pl.BlockSpec(memory_space=pl.ANY)
    in_vmem = pl.BlockSpec(memory_space=pltpu.VMEM)
    gathered, shared, own_solved, partial = pl.pallas_call(
        functools.partial(gather_and_solve, rows, layers, lanes, parts),
        out_shape=(
            jax.ShapeDtypeStruct((cols * depth, across), factor_panels.dtype),
            jax.ShapeDtypeStruct((panels * width, count), jnp.bfloat16),
            jax.ShapeDtypeStruct((width, count), jnp.float32),
            jax.ShapeDtypeStruct((layers * depth, count), jnp.float32),
        ),
        in_specs=[anywhere, anywhere, anywhere],
        out_specs=(anywhere, in_vmem, in_vmem, in_vmem),
        scratch_shapes=[
            pltpu.VMEM(inverse_blocks.shape, inverse_blocks.dtype),
            pltpu.VMEM((panels, width, count), right_sides.dtype),
            pltpu.VMEM((panels - 1, width, (panels - 1) * width), factor_panels.dtype),
            pltpu.VMEM((2, depth, across), factor_panels.dtype),
            pltpu.VMEM((2, depth, count), right_sides.dtype),
            dma((4, cols, parts)), dma((cols, parts)),
            dma((rows,)), dma((panels,)), dma((rows, parts)), dma((panels, parts)), dma((8,)),
        ],
        compiler_params=pltpu.CompilerParams(
            collective_id=0, has_side_effects=True, vmem_limit_bytes=16 << 20
        ),
    )(right_sides, factor_panels, inverse_blocks)

    return pl.pallas_call(
        functools.partial(multiply, panels, layers, lanes),
        out_shape=jax.ShapeDtypeStruct((height, count), jnp.float32),
        in_specs=[in_vmem] * 5,
        out_specs=anywhere,
        scratch_shapes=[pltpu.VMEM((2, depth, count), jnp.float32), dma((2,)), dma((layers,))],
        compiler_params=pltpu.CompilerParams(vmem_limit_bytes=16 << 20),
    )(right_sides, gathered, shared, own_solved, partial)


def solution(mesh):
    rows, cols = mesh.shape["row"], mesh.shape["col"]
    lanes = max(1, rows // 2)
    placed = (P("row", "col"), P(("row", "col"), None), P())
    return jax.shard_map(
        functools.partial(per_device, rows, cols // lanes, lanes),
        mesh=mesh, in_specs=placed, out_specs=P("row", "col"), check_vma=False,
    )
```
